32 devices in a mesh: section: 2 (over y), ctx: 4 (over x, core), tensor: 4 (over z).
Axes of the slice: x: 2, y: 2, z: 4, core: 2. Of those that a mesh axis runs over, the one named last changes fastest.
Arguments:
- arriving: bfloat16 [2, 1024, 4096], P('section', 'ctx', 'tensor')
- stored: bfloat16 [2, 1024, 4096], P('section', 'ctx', 'tensor')
- docs_forward: int32 [2, 1024], P('section', 'ctx'), may hold values from 0 to 3, never falling along the last dimension, each value on 1 to 512 neighbouring positions
- docs_backward: int32 [2, 1024], P('section', 'ctx'), may hold values from 0 to 3, never falling along the last dimension, each value on 1 to 512 neighbouring positions
- norm_gain: bfloat16 [2, 4096], P('section')
- query_weight: bfloat16 [2, 4096, 4096], P('section', 'ctx', 'tensor')
- key_weight: bfloat16 [2, 4096, 512], P('section', 'ctx', 'tensor')
- value_projection_weight: bfloat16 [2, 4096, 512], P('section', 'ctx', 'tensor'), may hold values from -0.09375 to 0.09375
- out_weight: bfloat16 [2, 4096, 4096], P('section', 'tensor', 'ctx'), may hold values from -0.375 to 0.375
Outputs:
- forward_output: bfloat16 [2, 1024, 4096], P('section', 'ctx', 'tensor')
- stashed: bfloat16 [2, 1024, 4096], P('section', 'ctx', 'tensor')
- rebuilt: bfloat16 [2, 1024, 4096], P('section', 'ctx', 'tensor')
The draws below stay inside these ranges and needn't reach their ends.
Inputs may be any that keep to these rules, and one draw needn't show every extreme that they name: `docs_forward`: each row holds 4 packed documents: ids never fall, each document has 1 to 512 tokens, one exactly 512. `docs_backward`: each row holds 4 packed documents: ids never fall, each document has 1 to 512 tokens, one exactly 512.
All inputs are finite; a program needn't handle non-finite values.
Results may differ from the reference program's by a relative error of at most 0.0066.
Values may be sent and summed in bfloat16 or wider, within the bound.
A program may use at most 128 MiB of HBM per device.

```python
import math
import jax
import jax.numpy as jnp
import numpy as np
from jax import lax

MODEL_WIDTH = 4096
HEAD = 128
QH = 32
KVH = 4
DOCS = 4
HQ = 4096
KEY_FEATURES = 512
SEQ = 1024
RELAY_SECTIONS = 2
DOC_MOST = 512


def activation_draw(base_key):
    keys_list = jax.random.split(base_key, 3)
    shape_full = (RELAY_SECTIONS, SEQ, MODEL_WIDTH)
    noise_values = jnp.clip(jax.random.normal(keys_list[0], shape_full, jnp.float32), -4.0, 4.0)
    row_scale = jnp.exp(jax.random.uniform(keys_list[1], (RELAY_SECTIONS, SEQ, 1), jnp.float32, math.log(0.5), math.log(2.0)))
    column_scale = jnp.exp(jax.random.uniform(keys_list[2], (1, 1, MODEL_WIDTH), jnp.float32, math.log(0.7), math.log(1.4)))
    return (noise_values * row_scale * column_scale).astype(jnp.bfloat16)


def draw_arriving(key, part):
    return activation_draw(jax.random.fold_in(key, 1))


def draw_stored(key, part):
    return activation_draw(jax.random.fold_in(key, 2))


def draw_norm_gain(key, part):
    gain_key = jax.random.fold_in(key, 3)
    return jax.random.uniform(gain_key, (RELAY_SECTIONS, MODEL_WIDTH), jnp.float32, 0.6, 1.6).astype(jnp.bfloat16)


def key_base(key):
    noise_values = jnp.clip(jax.random.normal(jax.random.fold_in(key, 31), (RELAY_SECTIONS, MODEL_WIDTH, KVH * HEAD), jnp.float32), -4.0, 4.0)
    return noise_values * (1.0 / math.sqrt(MODEL_WIDTH))


def draw_key_weight(key, part):
    return key_base(key).astype(jnp.bfloat16)


def draw_query_weight(key, part):
    noise_values = jnp.clip(jax.random.normal(jax.random.fold_in(key, 32), (RELAY_SECTIONS, MODEL_WIDTH, QH * HEAD), jnp.float32), -4.0, 4.0) * (1.0 / math.sqrt(MODEL_WIDTH))
    return noise_values.astype(jnp.bfloat16)


def shard_levels(stream_key, extent, pieces, smallest, largest):
    def one(axis_at, parts):
        heights = jax.random.uniform(jax.random.fold_in(jax.random.fold_in(stream_key, 6), axis_at), (parts,), jnp.float32, smallest / len(pieces), largest / len(pieces))
        return jnp.repeat(jnp.exp(heights), extent[axis_at] // parts).reshape((-1,) + (1,) * (len(extent) - axis_at - 1))

    factor_of = one(*pieces[0])
    for cut in pieces[1:]:
        factor_of = factor_of * one(*cut)
    return factor_of


def split_up(count, total, limit, skew):
    loads = [(1 << 20) // math.isqrt(standing ** skew) + 1 for standing in range(2, count + 1)]
    surplus, given = total - limit - (count - 1), [1] * (count - 1)
    while surplus > 0:
        candidates = [i for i in range(count - 1) if given[i] < limit]
        mass, remaining = sum([loads[i] for i in candidates]), surplus
        for i in candidates:
            addition = min(limit - given[i], max(1, remaining * loads[i] // mass), surplus)
            given[i] = given[i] + addition
            surplus = surplus - addition
    return np.array([limit] + given)


def ragged(key, amount, total, limit, skew):
    if amount == 2:
        one = jax.random.randint(key, (), max(1, total - limit), min(limit, total - 1) + 1)
        return jnp.stack([one, total - one])
    lengths = jnp.asarray(split_up(amount, total, limit, skew), jnp.int32)
    twos = (amount - 1) // 2
    donor, sink = lengths[1:1 + 2 * twos:2], lengths[2:2 + 2 * twos:2]
    slack = jnp.minimum(donor - 1, limit - sink)
    shifted = jax.random.randint(jax.random.fold_in(key, 1), (twos,), 0, 1 << 20) % (slack + 1)
    lengths = lengths.at[1:1 + 2 * twos:2].set(donor - shifted).at[2:2 + 2 * twos:2].set(sink + shifted)
    return lengths[jax.random.permutation(jax.random.fold_in(key, 2), amount)]


def scatter_about(key, shape, deviation, limit, shards=(), kind=jnp.bfloat16):
    array = deviation * jax.random.normal(key, shape, jnp.float32)
    if shards:
        array = array * shard_levels(key, shape, shards, -0.22, 0.18)
    return jnp.clip(array, -limit, limit).astype(kind)


def setup_inputs(seed: int = 0) -> dict:
    streams_of = jax.random.split(jax.random.key(seed), 10)
    arriving = draw_arriving(jax.random.fold_in(streams_of[9], 71), 0)
    stored = draw_stored(jax.random.fold_in(streams_of[9], 71), 0)
    docs_forward = jax.vmap(lambda own: jnp.searchsorted(jnp.cumsum(ragged(own, DOCS, SEQ, DOC_MOST, 2)), jnp.arange(SEQ), side="right"))(jax.random.split(streams_of[2], RELAY_SECTIONS)).reshape((RELAY_SECTIONS, SEQ)).astype(jnp.int32)
    docs_backward = jax.vmap(lambda own: jnp.searchsorted(jnp.cumsum(ragged(own, DOCS, SEQ, DOC_MOST, 2)), jnp.arange(SEQ), side="right"))(jax.random.split(streams_of[3], RELAY_SECTIONS)).reshape((RELAY_SECTIONS, SEQ)).astype(jnp.int32)
    norm_gain = draw_norm_gain(jax.random.fold_in(streams_of[9], 71), 0)
    query_weight = draw_query_weight(jax.random.fold_in(streams_of[9], 71), 0)
    key_weight = draw_key_weight(jax.random.fold_in(streams_of[9], 71), 0)
    value_projection_weight = scatter_about(streams_of[7], (RELAY_SECTIONS, MODEL_WIDTH, KEY_FEATURES), MODEL_WIDTH ** -0.5, 0.09375, ((0, 2), (1, 4), (2, 4)))
    out_weight = scatter_about(streams_of[8], (RELAY_SECTIONS, HQ, MODEL_WIDTH), (HQ // 16) ** -0.5, 0.375, ((0, 2), (1, 4), (2, 4)))
    return {"arriving": arriving, "stored": stored, "docs_forward": docs_forward, "docs_backward": docs_backward, "norm_gain": norm_gain, "query_weight": query_weight, "key_weight": key_weight, "value_projection_weight": value_projection_weight, "out_weight": out_weight}


norm_epsilon = 1e-05
rope_base = 500000.0

def normalize(inputs, gain_row):
    values = inputs.astype(jnp.float32)
    mean_square = lax.optimization_barrier(jnp.mean(values * values, axis=-1, keepdims=True))
    return (values * lax.rsqrt(mean_square + norm_epsilon) * gain_row.astype(jnp.float32)).astype(jnp.bfloat16)

def rotary(values, positions, head_size):
    half_size = head_size // 2
    tokens = values.shape[0]
    shaped = values.reshape(tokens, -1, head_size)
    exponent = jnp.arange(half_size).astype(jnp.float32) * (2.0 / head_size)
    inverse = jnp.exp(-exponent * math.log(rope_base))
    angles = positions.astype(jnp.float32)[:, None] * inverse[None, :]
    cosine_lookup = jnp.cos(angles)[:, None, :]
    sine_table = jnp.sin(angles)[:, None, :]
    first_half = shaped[:, :, :half_size]
    second_half = shaped[:, :, half_size:]
    turned = jnp.concatenate((first_half * cosine_lookup - second_half * sine_table, second_half * cosine_lookup + first_half * sine_table), axis=2)
    return turned.reshape(tokens, -1)

def attend(queries, key_rows, value_rows, positions, doc_ids):
    token_count = queries.shape[0]
    group_count = key_rows.shape[1] // HEAD
    group_size = QH // KVH
    permitted_mask = (positions[None, :] <= positions[:, None]) & (doc_ids[None, :] == doc_ids[:, None])
    grouped = queries.reshape(token_count, group_count, group_size, HEAD).astype(jnp.float32)
    key_heads = key_rows.reshape(token_count, group_count, HEAD).astype(jnp.float32)
    value_heads = value_rows.reshape(token_count, group_count, HEAD).astype(jnp.float32)

    def one_group(operands):
        group_queries, group_keys, group_values = operands
        scores = jnp.einsum('qgh,sh->gqs', group_queries, group_keys) * (1.0 / math.sqrt(HEAD))
        masked = jnp.where(permitted_mask[None], scores, -jnp.inf)
        row_peak = lax.optimization_barrier(jnp.max(masked, axis=2, keepdims=True))
        weights = jnp.exp(masked - row_peak)
        totals = lax.optimization_barrier(jnp.sum(weights, axis=2, keepdims=True))
        probabilities = weights.astype(jnp.bfloat16).astype(jnp.float32)
        mixed_heads = jnp.einsum('gqs,sh->gqh', probabilities, group_values) / totals
        return mixed_heads
    outputs = lax.map(one_group, (jnp.transpose(grouped, (1, 0, 2, 3)), jnp.transpose(key_heads, (1, 0, 2)), jnp.transpose(value_heads, (1, 0, 2))))
    return jnp.transpose(outputs, (2, 0, 1, 3)).reshape(token_count, -1).astype(jnp.bfloat16)

def apply_layer(operands):
    inputs, doc_ids, gain_row, query_matrix, key_matrix, value_matrix, out_matrix = operands
    normed = normalize(inputs, gain_row)
    positions = jnp.arange(SEQ).astype(jnp.int32)
    queries = rotary(jnp.dot(normed, query_matrix, preferred_element_type=jnp.float32), positions, HEAD).astype(jnp.bfloat16)
    key_rows = rotary(jnp.dot(normed, key_matrix, preferred_element_type=jnp.float32), positions, HEAD).astype(jnp.bfloat16)
    value_rows = jnp.dot(normed, value_matrix, preferred_element_type=jnp.float32).astype(jnp.bfloat16)
    mixed_heads = attend(queries, key_rows, value_rows, positions, doc_ids)
    summed = jnp.dot(mixed_heads, out_matrix, preferred_element_type=jnp.float32)
    return (inputs.astype(jnp.float32) + summed).astype(jnp.bfloat16)

def reference(arriving, stored, docs_forward, docs_backward, norm_gain, query_weight, key_weight, value_projection_weight, out_weight):
    forward_output = lax.map(apply_layer, (arriving, docs_forward, norm_gain, query_weight, key_weight, value_projection_weight, out_weight))
    stashed = jnp.roll(arriving, RELAY_SECTIONS // 2, axis=0)
    fetched = jnp.roll(stored, RELAY_SECTIONS // 2, axis=0)
    rebuilt = lax.map(apply_layer, (fetched, docs_backward, norm_gain, query_weight, key_weight, value_projection_weight, out_weight))
    return (forward_output, stashed, rebuilt)
```

```python
import math

import jax
import jax.numpy as jnp
import numpy as np
from jax import lax
from jax.experimental import pallas as pl
from jax.experimental.pallas import tpu as pltpu
from jax.sharding import PartitionSpec as P

HEAD = 128
DOC_MOST = 512
norm_epsilon = 1e-05
rope_base = 500000.0
MESH = pl.DeviceIdType.MESH
F32 = jnp.float32
BF16 = jnp.bfloat16
Q_PIECES = 4
O_PIECES = 4


def layer_kernel(
    sections,
    n_ctx,
    n,
    arr,
    sto,
    docs_rows,
    docs_cols,
    gain,
    wq,
    wk,
    wv,
    wo,
    cos_all,
    sin_all,
    out_f,
    out_s,
    out_b,
    xg,
    wq_g,
    wkv_g,
    wo_g,
    normed,
    qs,
    mixed,
    kv_g,
    docs_g,
    cos_t,
    sin_t,
    pf,
    rs_out,
    rl,
    rr,
    local_sem,
    y_s,
    y_r,
    ag_s,
    ag_r,
    x_s,
    x_r,
    c_s,
    c_r,
    f_s,
    f_r,
    rs_s,
    rs_r,
):
    s = lax.axis_index("section")
    i = lax.axis_index("ctx")
    t = lax.axis_index("tensor")
    rows = arr.shape[1]
    width = arr.shape[2]
    depth = wq.shape[1]
    heads = wq.shape[2] // HEAD
    half = sections // 2
    partner = lax.rem(s + half, sections)
    across = lax.rem(i + n_ctx // 2, n_ctx)
    sibling = i + 1 - 2 * lax.rem(i, 2)
    has_left = t > 0
    has_right = t < n - 1

    barrier = pltpu.get_barrier_semaphore()
    pl.semaphore_signal(barrier, inc=1, device_id={"section": partner}, device_id_type=MESH)
    pl.semaphore_signal(barrier, inc=1, device_id={"ctx": across}, device_id_type=MESH)
    pl.semaphore_signal(barrier, inc=1, device_id={"ctx": sibling}, device_id_type=MESH)

    @pl.when(has_left)
    def _():
        pl.semaphore_signal(barrier, inc=1, device_id={"tensor": t - 1}, device_id_type=MESH)

    @pl.when(has_right)
    def _():
        pl.semaphore_signal(barrier, inc=1, device_id={"tensor": t + 1}, device_id_type=MESH)

    q_rows = depth // Q_PIECES
    o_rows = wo.shape[1] // O_PIECES
    locals_ = [
        (arr.at[0], xg.at[0, t]),
        (wk.at[0], wkv_g.at[i, :, pl.ds(0, HEAD)]),
        (wv.at[0], wkv_g.at[i, :, pl.ds(HEAD, HEAD)]),
        (wq.at[0], wq_g.at[i]),
        (wo.at[0], wo_g.at[i]),
        (docs_rows, docs_g.at[i]),
        (cos_all.at[pl.ds(pl.multiple_of(i * rows, rows), rows)], cos_t),
        (sin_all.at[pl.ds(pl.multiple_of(i * rows, rows), rows)], sin_t),
    ]
    local_copies = [
        pltpu.make_async_copy(a, b, local_sem.at[k]) for k, (a, b) in enumerate(locals_)
    ]
    for copy in local_copies:
        copy.start()

    pl.semaphore_wait(
        barrier, 3 + has_left.astype(jnp.int32) + has_right.astype(jnp.int32)
    )

    def remote(src, dst, send, recv, where):
        return pltpu.make_async_remote_copy(
            src_ref=src,
            dst_ref=dst,
            send_sem=send,
            recv_sem=recv,
            device_id=where,
            device_id_type=MESH,
        )

    pieces = [
        (docs_rows, lambda j: docs_g.at[j]),
        (wk.at[0], lambda j: wkv_g.at[j, :, pl.ds(0, HEAD)]),
        (wv.at[0], lambda j: wkv_g.at[j, :, pl.ds(HEAD, HEAD)]),
    ]
    for k in range(Q_PIECES):
        part = pl.ds(k * q_rows, q_rows)
        pieces.append((wq.at[0, part], lambda j, part=part: wq_g.at[j, part]))
    first_o = len(pieces)
    for k in range(O_PIECES):
        part = pl.ds(k * o_rows, o_rows)
        pieces.append((wo.at[0, part], lambda j, part=part: wo_g.at[j, part]))
    kv_piece = len(pieces)
    pieces.append((kv_g.at[i], lambda j: kv_g.at[j]))

    def to_across(p):
        src, slot = pieces[p]
        return remote(src, slot(i), x_s.at[p], x_r.at[p], {"ctx": across})

    def to_sibling(p):
        src, slot = pieces[p]
        return remote(src, slot(i), c_s.at[p], c_r.at[p], {"ctx": sibling})

    def passed_on(p):
        _, slot = pieces[p]
        return remote(slot(across), slot(across), f_s.at[p], f_r.at[p], {"ctx": sibling})

    def pass_on(p):
        to_across(p).wait_recv()
        passed_on(p).start()

    def arrived(p):
        to_sibling(p).wait_recv()
        passed_on(p).wait_recv()

    def ag_right(b, r):
        j = jnp.maximum(t - r, 0)
        src = arr.at[0] if (b == 0 and r == 0) else xg.at[b, j]
        return remote(src, xg.at[b, j], ag_s.at[0, b, r], ag_r.at[0, b, r], {"tensor": t + 1})

    def ag_left(b, r):
        j = jnp.minimum(t + r, n - 1)
        src = arr.at[0] if (b == 0 and r == 0) else xg.at[b, j]
        return remote(src, xg.at[b, j], ag_s.at[1, b, r], ag_r.at[1, b, r], {"tensor": t - 1})

    def sends_right(r):
        return has_right & (t >= r)

    def sends_left(r):
        return has_left & (t + r <= n - 1)

    def ag_start(b, r):
        @pl.when(sends_right(r))
        def _():
            ag_right(b, r).start()

        @pl.when(sends_left(r))
        def _():
            ag_left(b, r).start()

    def ag_wait(b, r):
        @pl.when(t - 1 - r >= 0)
        def _():
            ag_right(b, r).wait_recv()

        @pl.when(t + 1 + r <= n - 1)
        def _():
            ag_left(b, r).wait_recv()

    fetch = remote(sto.at[0], xg.at[1, t], y_s.at[0], y_r.at[0], {"section": partner})
    stash = remote(arr.at[0], out_s.at[0], y_s.at[1], y_r.at[1], {"section": partner})

    fetch.start()
    ag_start(0, 0)
    for p in range(first_o):
        to_across(p).start()
    for p in range(first_o):
        to_sibling(p).start()
    fetch.wait_recv()
    ag_start(1, 0)
    stash.start()
    for r in range(n - 2):
        for b in range(2):
            ag_wait(b, r)
            ag_start(b, r + 1)
    pass_on(0)
    pass_on(1)
    pass_on(2)
    half_q = 3 + Q_PIECES // 2
    for p in range(3, half_q):
        pass_on(p)
    for p in range(first_o, kv_piece):
        to_across(p).start()
    for copy in local_copies:
        copy.wait()

    def normalize(b):
        def step(k, carry):
            part = pl.ds(pl.multiple_of(k * 16, 16), 16)
            square = jnp.zeros((16, 1), F32)
            for j in range(n):
                v = xg[b, j, part, :].astype(F32)
                square = square + jnp.sum(v * v, axis=1, keepdims=True)
            factor = lax.rsqrt(square * (1.0 / (n * width)) + norm_epsilon)
            place = pl.ds(pl.multiple_of(b * rows + k * 16, 16), 16)
            for j in range(n):
                v = xg[b, j, part, :].astype(F32)
                g = gain[:, j * width : (j + 1) * width].astype(F32)
                normed[place, j * width : (j + 1) * width] = (v * factor * g).astype(BF16)
            return carry

        lax.fori_loop(0, rows // 16, step, 0)

    ag_wait(0, n - 2)
    normalize(0)
    for p in range(half_q, first_o):
        pass_on(p)
    for p in range(first_o, kv_piece):
        to_sibling(p).start()
    ag_wait(1, n - 2)
    normalize(1)
    for p in range(first_o):
        arrived(p)

    def rotated(u):
        both = []
        for b in range(2):
            v = u[b * rows : (b + 1) * rows]
            both.append(v * cos_t[...] + pltpu.roll(v, HEAD // 2, 1) * sin_t[...])
        return both

    k_and_v = jnp.zeros((2 * rows, 2 * HEAD), F32)
    for j in range(n_ctx):
        k_and_v = k_and_v + jnp.dot(
            normed[:, j * depth : (j + 1) * depth], wkv_g[j], preferred_element_type=F32
        )
    for b, v in enumerate(rotated(k_and_v[:, :HEAD])):
        kv_g[i, b, :, :HEAD] = v.astype(BF16)
        kv_g[i, b, :, HEAD:] = k_and_v[b * rows : (b + 1) * rows, HEAD:].astype(BF16)
    to_across(kv_piece).start()
    to_sibling(kv_piece).start()

    def q_step(c, carry):
        cols = pl.ds(pl.multiple_of(c * 2 * HEAD, 2 * HEAD), 2 * HEAD)
        acc = jnp.zeros((2 * rows, 2 * HEAD), F32)
        for j in range(n_ctx):
            acc = acc + jnp.dot(
                normed[:, j * depth : (j + 1) * depth],
                wq_g[j, :, cols],
                preferred_element_type=F32,
            )
        for h in range(2):
            place = pl.ds(pl.multiple_of((c * 2 + h) * HEAD, HEAD), HEAD)
            for b, v in enumerate(rotated(acc[:, h * HEAD : (h + 1) * HEAD])):
                qs[b * rows : (b + 1) * rows, place] = v.astype(BF16)
        return carry

    lax.fori_loop(0, heads // 2, q_step, 0)
    pass_on(kv_piece)
    for p in range(first_o, first_o + O_PIECES // 2):
        pass_on(p)
    arrived(kv_piece)

    blocks = min(n_ctx, -(-(DOC_MOST - 1) // rows) + 1)
    start = jnp.maximum(i - (blocks - 1), 0)
    keys = blocks * rows
    q_pos = i * rows + lax.broadcasted_iota(jnp.int32, (rows, keys), 0)
    k_pos = start * rows + lax.broadcasted_iota(jnp.int32, (rows, keys), 1)
    causal = k_pos <= q_pos
    for b in range(2):
        key_docs = jnp.concatenate([docs_g[start + j, b] for j in range(blocks)], axis=1)
        allowed = causal & (docs_cols[b] == key_docs[:1])
        k_b = jnp.concatenate([kv_g[start + j, b, :, :HEAD] for j in range(blocks)], axis=0)
        v_b = jnp.concatenate([kv_g[start + j, b, :, HEAD:] for j in range(blocks)], axis=0)

        def head_step(h, carry):
            place = pl.ds(pl.multiple_of(h * HEAD, HEAD), HEAD)
            q_h = qs[b * rows : (b + 1) * rows, place]
            scores = lax.dot_general(
                q_h, k_b, (((1,), (1,)), ((), ())), preferred_element_type=F32
            ) * (1.0 / math.sqrt(HEAD))
            masked = jnp.where(allowed, scores, -jnp.inf)
            peak = jnp.max(masked, axis=1, keepdims=True)
            weights = jnp.exp(masked - peak)
            total = jnp.sum(weights, axis=1, keepdims=True)
            mix = jnp.dot(weights.astype(BF16), v_b, preferred_element_type=F32)
            mixed[b * rows : (b + 1) * rows, place] = (mix / total).astype(BF16)
            return carry

        lax.fori_loop(0, heads, head_step, 0)
        if b == 0:
            pass_on(first_o + O_PIECES // 2)
    for p in range(first_o + O_PIECES // 2 + 1, kv_piece):
        pass_on(p)
    for p in range(first_o, kv_piece):
        arrived(p)

    def project(k):
        d = jnp.where(t < n // 2, n - 1 - k, k)

        def step(c, carry):
            cols = pl.ds(pl.multiple_of(c * 256, 256), 256)
            pf[d, :, cols] = jnp.dot(mixed[...], wo_g[d, :, cols], preferred_element_type=F32)
            return carry

        lax.fori_loop(0, width // 256, step, 0)

    def rs_right(r, b, d):
        return remote(
            rs_out.at[d, b], rl.at[d, b], rs_s.at[0, r, b], rs_r.at[0, r, b], {"tensor": t + 1}
        )

    def rs_left(r, b, d):
        return remote(
            rs_out.at[d, b], rr.at[d, b], rs_s.at[1, r, b], rs_r.at[1, r, b], {"tensor": t - 1}
        )

    def dest_right(r):
        return jnp.minimum(n - 1 + t - r, n - 1)

    def dest_left(r):
        return jnp.maximum(r - (n - 1 - t), 0)

    def rs_round(r):
        for b in range(2):
            part = pl.ds(b * rows, rows)

            @pl.when(has_right & (r >= t))
            def _():
                d = dest_right(r)

                @pl.when(has_left)
                def _():
                    if r > 0:
                        rs_right(r - 1, b, d).wait_recv()
                        rs_out[d, b] = (pf[d, part, :] + rl[d, b].astype(F32)).astype(BF16)

                @pl.when(jnp.logical_not(has_left))
                def _():
                    rs_out[d, b] = pf[d, part, :].astype(BF16)

                rs_right(r, b, d).start()

            @pl.when(has_left & (r >= n - 1 - t))
            def _():
                d = dest_left(r)

                @pl.when(has_right)
                def _():
                    if r > 0:
                        rs_left(r - 1, b, d).wait_recv()
                        rs_out[d, b] = (pf[d, part, :] + rr[d, b].astype(F32)).astype(BF16)

                @pl.when(jnp.logical_not(has_right))
                def _():
                    rs_out[d, b] = pf[d, part, :].astype(BF16)

                rs_left(r, b, d).start()

    for r in range(n - 1):
        project(r)
        if r == n - 2:
            project(n - 1)
        rs_round(r)

    for b, out in enumerate((out_f, out_b)):
        part = pl.ds(b * rows, rows)

        @pl.when(has_left)
        def _():
            rs_right(n - 2, b, t).wait_recv()
            pf[t, part, :] = pf[t, part, :] + rl[t, b].astype(F32)

        @pl.when(has_right)
        def _():
            rs_left(n - 2, b, t).wait_recv()
            pf[t, part, :] = pf[t, part, :] + rr[t, b].astype(F32)

        out[0] = (xg[b, t].astype(F32) + pf[t, part, :]).astype(BF16)

    stash.wait_recv()
    fetch.wait_send()
    stash.wait_send()
    for p in range(len(pieces)):
        to_across(p).wait_send()
        to_sibling(p).wait_send()
        passed_on(p).wait_send()
    for r in range(n - 1):
        for b in range(2):

            @pl.when(sends_right(r))
            def _():
                ag_right(b, r).wait_send()

            @pl.when(sends_left(r))
            def _():
                ag_left(b, r).wait_send()

            @pl.when(has_right & (r >= t))
            def _():
                rs_right(r, b, dest_right(r)).wait_send()

            @pl.when(has_left & (r >= n - 1 - t))
            def _():
                rs_left(r, b, dest_left(r)).wait_send()


def rope_tables(tokens):
    exponent = np.arange(HEAD // 2, dtype=np.float64) * (2.0 / HEAD)
    angles = np.arange(tokens, dtype=np.float64)[:, None] * rope_base ** -exponent[None, :]
    cosine, sine = np.cos(angles), np.sin(angles)
    return (
        np.concatenate((cosine, cosine), axis=1).astype(np.float32),
        np.concatenate((-sine, sine), axis=1).astype(np.float32),
    )


def solution(mesh):
    sections, n_ctx, n = (mesh.shape[a] for a in ("section", "ctx", "tensor"))

    def body(arr, sto, docs_f, docs_b, gain, wq, wk, wv, wo):
        rows, width = arr.shape[1:]
        depth, qw = wq.shape[1:]
        odepth, ow = wo.shape[1:]
        pair = jnp.stack((docs_f[0], docs_b[0]), axis=0)
        docs_rows = jnp.broadcast_to(pair[:, None, :], (2, 8, rows))
        docs_cols = pair[:, :, None]
        cosine, sine = rope_tables(rows * n_ctx)
        n_pieces = 3 + Q_PIECES + O_PIECES + 1
        hbm = pl.BlockSpec(memory_space=pl.ANY)
        vmem = pl.BlockSpec(memory_space=pltpu.VMEM)
        dma = pltpu.SemaphoreType.DMA
        block = jax.ShapeDtypeStruct((1, rows, width), BF16)

        def kernel(*refs):
            layer_kernel(sections, n_ctx, n, *refs)

        return pl.pallas_call(
            kernel,
            out_shape=(block, block, block),
            in_specs=[hbm, hbm, hbm, vmem, vmem] + [hbm] * 6,
            out_specs=(vmem, hbm, vmem),
            scratch_shapes=[
                pltpu.VMEM((2, n, rows, width), BF16),
                pltpu.VMEM((n_ctx, depth, qw), BF16),
                pltpu.VMEM((n_ctx, depth, 2 * HEAD), BF16),
                pltpu.VMEM((n_ctx, odepth, ow), BF16),
                pltpu.VMEM((2 * rows, n * width), BF16),
                pltpu.VMEM((2 * rows, qw), BF16),
                pltpu.VMEM((2 * rows, qw), BF16),
                pltpu.VMEM((n_ctx, 2, rows, 2 * HEAD), BF16),
                pltpu.VMEM((n_ctx, 2, 8, rows), jnp.int32),
                pltpu.VMEM((rows, HEAD), F32),
                pltpu.VMEM((rows, HEAD), F32),
                pltpu.VMEM((n, 2 * rows, width), F32),
                pltpu.VMEM((n, 2, rows, width), BF16),
                pltpu.VMEM((n, 2, rows, width), BF16),
                pltpu.VMEM((n, 2, rows, width), BF16),
                dma((8,)),
                dma((2,)),
                dma((2,)),
                dma((2, 2, n - 1)),
                dma((2, 2, n - 1)),
                dma((n_pieces,)),
                dma((n_pieces,)),
                dma((n_pieces,)),
                dma((n_pieces,)),
                dma((n_pieces,)),
                dma((n_pieces,)),
                dma((2, n - 1, 2)),
                dma((2, n - 1, 2)),
            ],
            compiler_params=pltpu.CompilerParams(
                collective_id=0, has_side_effects=True, vmem_limit_bytes=62 * 1024 * 1024
            ),
            cost_estimate=pl.CostEstimate(
                flops=2 * 2 * rows * n * width * (2 * qw + 2 * HEAD),
                bytes_accessed=16 * 1024 * 1024,
                transcendentals=8 * 2 * rows * 768,
            ),
            name="relay_layer",
        )(arr, sto, docs_rows, docs_cols, gain, wq, wk, wv, wo, cosine, sine)

    return jax.shard_map(
        body,
        mesh=mesh,
        in_specs=(
            P("section", "ctx", "tensor"),
            P("section", "ctx", "tensor"),
            P("section", "ctx"),
            P("section", "ctx"),
            P("section", None),
            P("section", "ctx", "tensor"),
            P("section", "ctx", "tensor"),
            P("section", "ctx", "tensor"),
            P("section", "tensor", "ctx"),
        ),
        out_specs=(
            P("section", "ctx", "tensor"),
            P("section", "ctx", "tensor"),
            P("section", "ctx", "tensor"),
        ),
        check_vma=False,
    )
```

```python
import math

import jax
import jax.numpy as jnp
import numpy as np
from jax import lax
from jax.experimental import pallas as pl
from jax.experimental.pallas import tpu as pltpu
from jax.sharding import PartitionSpec as P

HEAD = 128
DOC_MOST = 512
norm_epsilon = 1e-05
rope_base = 500000.0
MESH = pl.DeviceIdType.MESH
F32 = jnp.float32
BF16 = jnp.bfloat16
Q_PIECES = 4
O_PIECES = 4
SUM_PARTS = 2


def layer_kernel(
    sections,
    n_ctx,
    n,
    arr,
    sto,
    docs_rows,
    docs_cols,
    gain,
    wq,
    wk,
    wv,
    wo,
    cos_all,
    sin_all,
    out_f,
    out_s,
    out_b,
    xg,
    wq_g,
    wkv_g,
    wo_g,
    normed,
    qs,
    mixed,
    kv_g,
    docs_g,
    cos_t,
    sin_t,
    pf,
    rs_out,
    rl,
    rr,
    res,
    local_sem,
    y_s,
    y_r,
    ag_s,
    ag_r,
    x_s,
    x_r,
    c_s,
    c_r,
    f_s,
    f_r,
    rs_s,
    rs_r,
):
    s = lax.axis_index("section")
    i = lax.axis_index("ctx")
    t = lax.axis_index("tensor")
    rows = arr.shape[1]
    width = arr.shape[2]
    depth = wq.shape[1]
    heads = wq.shape[2] // HEAD
    half = sections // 2
    parts_each = SUM_PARTS
    sum_rows = rows // SUM_PARTS
    partner = lax.rem(s + half, sections)
    across = lax.rem(i + n_ctx // 2, n_ctx)
    sibling = i + 1 - 2 * lax.rem(i, 2)
    has_left = t > 0
    has_right = t < n - 1

    barrier = pltpu.get_barrier_semaphore()
    pl.semaphore_signal(barrier, inc=1, device_id={"section": partner}, device_id_type=MESH)
    pl.semaphore_signal(barrier, inc=1, device_id={"ctx": across}, device_id_type=MESH)
    pl.semaphore_signal(barrier, inc=1, device_id={"ctx": sibling}, device_id_type=MESH)

    @pl.when(has_left)
    def _():
        pl.semaphore_signal(barrier, inc=1, device_id={"tensor": t - 1}, device_id_type=MESH)

    @pl.when(has_right)
    def _():
        pl.semaphore_signal(barrier, inc=1, device_id={"tensor": t + 1}, device_id_type=MESH)

    q_rows = depth // Q_PIECES
    o_rows = wo.shape[1] // O_PIECES
    locals_ = [
        (arr.at[0], xg.at[0, t]),
        (wk.at[0], wkv_g.at[i, :, pl.ds(0, HEAD)]),
        (wv.at[0], wkv_g.at[i, :, pl.ds(HEAD, HEAD)]),
        (wq.at[0], wq_g.at[i]),
        (wo.at[0], wo_g.at[i]),
        (docs_rows, docs_g.at[i]),
        (cos_all.at[pl.ds(pl.multiple_of(i * rows, rows), rows)], cos_t),
        (sin_all.at[pl.ds(pl.multiple_of(i * rows, rows), rows)], sin_t),
    ]
    local_copies = [
        pltpu.make_async_copy(a, b, local_sem.at[k]) for k, (a, b) in enumerate(locals_)
    ]
    for copy in local_copies:
        copy.start()

    pl.semaphore_wait(
        barrier, 3 + has_left.astype(jnp.int32) + has_right.astype(jnp.int32)
    )

    def remote(src, dst, send, recv, where):
        return pltpu.make_async_remote_copy(
            src_ref=src,
            dst_ref=dst,
            send_sem=send,
            recv_sem=recv,
            device_id=where,
            device_id_type=MESH,
        )

    pieces = [
        (docs_rows, lambda j: docs_g.at[j]),
        (wk.at[0], lambda j: wkv_g.at[j, :, pl.ds(0, HEAD)]),
        (wv.at[0], lambda j: wkv_g.at[j, :, pl.ds(HEAD, HEAD)]),
    ]
    for k in range(Q_PIECES):
        part = pl.ds(k * q_rows, q_rows)
        pieces.append((wq.at[0, part], lambda j, part=part: wq_g.at[j, part]))
    first_o = len(pieces)
    for k in range(O_PIECES):
        part = pl.ds(k * o_rows, o_rows)
        pieces.append((wo.at[0, part], lambda j, part=part: wo_g.at[j, part]))
    kv_piece = len(pieces)
    for b in range(2):
        pieces.append((kv_g.at[i, b], lambda j, b=b: kv_g.at[j, b]))

    def to_across(p):
        src, slot = pieces[p]
        return remote(src, slot(i), x_s.at[p], x_r.at[p], {"ctx": across})

    def to_sibling(p):
        src, slot = pieces[p]
        return remote(src, slot(i), c_s.at[p], c_r.at[p], {"ctx": sibling})

    def passed_on(p):
        _, slot = pieces[p]
        return remote(slot(across), slot(across), f_s.at[p], f_r.at[p], {"ctx": sibling})

    def pass_on(p):
        to_across(p).wait_recv()
        passed_on(p).start()

    def arrived(p):
        to_sibling(p).wait_recv()
        passed_on(p).wait_recv()

    def ag_right(b, r):
        j = jnp.maximum(t - r, 0)
        src = arr.at[0] if (b == 0 and r == 0) else xg.at[b, j]
        return remote(src, xg.at[b, j], ag_s.at[0, b, r], ag_r.at[0, b, r], {"tensor": t + 1})

    def ag_left(b, r):
        j = jnp.minimum(t + r, n - 1)
        src = arr.at[0] if (b == 0 and r == 0) else xg.at[b, j]
        return remote(src, xg.at[b, j], ag_s.at[1, b, r], ag_r.at[1, b, r], {"tensor": t - 1})

    def sends_right(r):
        return has_right & (t >= r)

    def sends_left(r):
        return has_left & (t + r <= n - 1)

    def ag_start(b, r):
        @pl.when(sends_right(r))
        def _():
            ag_right(b, r).start()

        @pl.when(sends_left(r))
        def _():
            ag_left(b, r).start()

    def ag_wait(b, r):
        @pl.when(t - 1 - r >= 0)
        def _():
            ag_right(b, r).wait_recv()

        @pl.when(t + 1 + r <= n - 1)
        def _():
            ag_left(b, r).wait_recv()

    fetch = remote(sto.at[0], xg.at[1, t], y_s.at[0], y_r.at[0], {"section": partner})
    stash = remote(arr.at[0], out_s.at[0], y_s.at[1], y_r.at[1], {"section": partner})

    fetch.start()
    ag_start(0, 0)
    for p in range(first_o):
        to_across(p).start()
    for p in range(kv_piece):
        to_sibling(p).start()
    fetch.wait_recv()
    ag_start(1, 0)
    stash.start()
    for r in range(n - 2):
        for b in range(2):
            ag_wait(b, r)
            ag_start(b, r + 1)
    def normalize(b):
        def step(k, carry):
            part = pl.ds(pl.multiple_of(k * 16, 16), 16)
            square = jnp.zeros((16, 1), F32)
            for j in range(n):
                v = xg[b, j, part, :].astype(F32)
                square = square + jnp.sum(v * v, axis=1, keepdims=True)
            factor = lax.rsqrt(square * (1.0 / (n * width)) + norm_epsilon)
            place = pl.ds(pl.multiple_of(b * rows + k * 16, 16), 16)
            for j in range(n):
                v = xg[b, j, part, :].astype(F32)
                g = gain[:, j * width : (j + 1) * width].astype(F32)
                normed[place, j * width : (j + 1) * width] = (v * factor * g).astype(BF16)
            return carry

        lax.fori_loop(0, rows // 16, step, 0)

    def rotated(v):
        return v * cos_t[...] + pltpu.roll(v, HEAD // 2, 1) * sin_t[...]

    def project_keys(b):
        own = slice(b * rows, (b + 1) * rows)
        k_and_v = jnp.zeros((rows, 2 * HEAD), F32)
        for j in range(n_ctx):
            k_and_v = k_and_v + jnp.dot(
                normed[own, j * depth : (j + 1) * depth], wkv_g[j], preferred_element_type=F32
            )
        kv_g[i, b, :, :HEAD] = rotated(k_and_v[:, :HEAD]).astype(BF16)
        kv_g[i, b, :, HEAD:] = k_and_v[:, HEAD:].astype(BF16)
        to_across(kv_piece + b).start()
        to_sibling(kv_piece + b).start()

    def project_queries(b):
        own = slice(b * rows, (b + 1) * rows)

        def q_step(c, carry):
            cols = pl.ds(pl.multiple_of(c * 2 * HEAD, 2 * HEAD), 2 * HEAD)
            acc = jnp.zeros((rows, 2 * HEAD), F32)
            for j in range(n_ctx):
                acc = acc + jnp.dot(
                    normed[own, j * depth : (j + 1) * depth],
                    wq_g[j, :, cols],
                    preferred_element_type=F32,
                )
            for h in range(2):
                place = pl.ds(pl.multiple_of((c * 2 + h) * HEAD, HEAD), HEAD)
                qs[own, place] = rotated(acc[:, h * HEAD : (h + 1) * HEAD]).astype(BF16)
            return carry

        lax.fori_loop(0, heads // 2, q_step, 0)

    blocks = min(n_ctx, -(-(DOC_MOST - 1) // rows) + 1)
    start = jnp.maximum(i - (blocks - 1), 0)
    keys = blocks * rows

    def attend(b):
        q_pos = i * rows + lax.broadcasted_iota(jnp.int32, (rows, keys), 0)
        k_pos = start * rows + lax.broadcasted_iota(jnp.int32, (rows, keys), 1)
        key_docs = jnp.concatenate([docs_g[start + j, b] for j in range(blocks)], axis=1)
        allowed = (k_pos <= q_pos) & (docs_cols[b] == key_docs[:1])
        k_b = jnp.concatenate([kv_g[start + j, b, :, :HEAD] for j in range(blocks)], axis=0)
        v_b = jnp.concatenate([kv_g[start + j, b, :, HEAD:] for j in range(blocks)], axis=0)

        def head_step(h, carry):
            place = pl.ds(pl.multiple_of(h * HEAD, HEAD), HEAD)
            q_h = qs[b * rows : (b + 1) * rows, place]
            scores = lax.dot_general(
                q_h, k_b, (((1,), (1,)), ((), ())), preferred_element_type=F32
            ) * (1.0 / math.sqrt(HEAD))
            masked = jnp.where(allowed, scores, -jnp.inf)
            peak = jnp.max(masked, axis=1, keepdims=True)
            weights = jnp.exp(masked - peak)
            total = jnp.sum(weights, axis=1, keepdims=True)
            mix = jnp.dot(weights.astype(BF16), v_b, preferred_element_type=F32)
            mixed[b * rows : (b + 1) * rows, place] = (mix / total).astype(BF16)
            return carry

        lax.fori_loop(0, heads, head_step, 0)

    n_half = n // 2
    x_half = i // (n_ctx // 2)
    near = x_half * n_half
    far = (1 - x_half) * n_half

    def project(b, base):
        own = slice(b * rows, (b + 1) * rows)

        def step(c, carry):
            d = base + c // (width // 256)
            cols = pl.ds(pl.multiple_of(lax.rem(c, width // 256) * 256, 256), 256)
            pf[d, own, cols] = jnp.dot(mixed[own, :], wo_g[d, :, cols], preferred_element_type=F32)
            return carry

        lax.fori_loop(0, n_half * (width // 256), step, 0)

    def part_of(m):
        return pl.ds(m * sum_rows, sum_rows)

    def rs_right(d, m):
        part = part_of(m)
        return remote(
            rs_out.at[d, part], rl.at[d, part], rs_s.at[0, d, m], rs_r.at[0, d, m], {"tensor": t + 1}
        )

    def rs_left(d, m):
        part = part_of(m)
        return remote(
            rs_out.at[d, part], rr.at[d, part], rs_s.at[1, d, m], rs_r.at[1, d, m], {"tensor": t - 1}
        )

    def pieces_of(b):
        return range(b * parts_each, (b + 1) * parts_each)

    def first_sends(b, base):
        for q in range(n_half):
            low, high = base + q, base + n_half - 1 - q

            @pl.when((t == n - 1) & (low < t))
            def _():
                for m in pieces_of(b):
                    rs_out[low, part_of(m), :] = pf[low, part_of(m), :].astype(BF16)
                    rs_left(low, m).start()

            @pl.when((t == 0) & (high > t))
            def _():
                for m in pieces_of(b):
                    rs_out[high, part_of(m), :] = pf[high, part_of(m), :].astype(BF16)
                    rs_right(high, m).start()

    def middle_sends(b, base, q):
        low, high = base + q, base + n_half - 1 - q

        @pl.when((t < n - 1) & (low < t))
        def _():
            for m in pieces_of(b):
                rs_left(low, m).wait_recv()
                rs_out[low, part_of(m), :] = (
                    pf[low, part_of(m), :] + rr[low, part_of(m), :].astype(F32)
                ).astype(BF16)
                rs_left(low, m).start()

        @pl.when((t > 0) & (high > t))
        def _():
            for m in pieces_of(b):
                rs_right(high, m).wait_recv()
                rs_out[high, part_of(m), :] = (
                    pf[high, part_of(m), :] + rl[high, part_of(m), :].astype(F32)
                ).astype(BF16)
                rs_right(high, m).start()

    for copy in local_copies:
        copy.wait()
    ag_wait(0, n - 2)
    normalize(0)
    for p in range(first_o):
        pass_on(p)
    for p in range(first_o):
        arrived(p)
    project_keys(0)
    project_queries(0)
    pass_on(kv_piece)
    to_across(first_o).start()
    arrived(kv_piece)
    attend(0)
    for p in range(first_o, kv_piece):
        to_sibling(p).wait_recv()
    project(0, near)
    first_sends(0, near)

    ag_wait(1, n - 2)
    normalize(1)
    project_keys(1)
    for p in range(first_o + 1, kv_piece):
        to_across(p).start()
    project_queries(1)
    pass_on(kv_piece + 1)
    arrived(kv_piece + 1)
    attend(1)
    project(1, near)
    first_sends(1, near)

    for q in range(n_half):
        middle_sends(0, near, q)
    pass_on(first_o)
    for p in range(first_o + 1, kv_piece):
        pass_on(p)
        if p - first_o - 1 < n_half:
            middle_sends(1, near, p - first_o - 1)
    for p in range(first_o, kv_piece):
        passed_on(p).wait_recv()
    for b in range(2):
        project(b, far)
        first_sends(b, far)
    for b in range(2):
        for q in range(n_half):
            middle_sends(b, far, q)

    outs = []
    for m in range(2 * parts_each):
        b, k = m // parts_each, m % parts_each
        part = part_of(m)

        @pl.when(has_left)
        def _():
            rs_right(t, m).wait_recv()
            pf[t, part, :] = pf[t, part, :] + rl[t, part, :].astype(F32)

        @pl.when(has_right)
        def _():
            rs_left(t, m).wait_recv()
            pf[t, part, :] = pf[t, part, :] + rr[t, part, :].astype(F32)

        own = pl.ds(k * sum_rows, sum_rows)
        res[part, :] = (xg[b, t, own, :].astype(F32) + pf[t, part, :]).astype(BF16)
        out = pltpu.make_async_copy(
            res.at[part], (out_f, out_b)[b].at[0, own], local_sem.at[len(locals_) + m]
        )
        out.start()
        outs.append(out)
    for out in outs:
        out.wait()

    stash.wait_recv()
    fetch.wait_send()
    stash.wait_send()
    for p in range(len(pieces)):
        to_across(p).wait_send()
        to_sibling(p).wait_send()
        passed_on(p).wait_send()
    for r in range(n - 1):
        for b in range(2):

            @pl.when(sends_right(r))
            def _():
                ag_right(b, r).wait_send()

            @pl.when(sends_left(r))
            def _():
                ag_left(b, r).wait_send()

    for d in range(n):

        @pl.when(d > t)
        def _():
            for m in range(2 * parts_each):
                rs_right(d, m).wait_send()

        @pl.when(d < t)
        def _():
            for m in range(2 * parts_each):
                rs_left(d, m).wait_send()


def rope_tables(tokens):
    exponent = np.arange(HEAD // 2, dtype=np.float64) * (2.0 / HEAD)
    angles = np.arange(tokens, dtype=np.float64)[:, None] * rope_base ** -exponent[None, :]
    cosine, sine = np.cos(angles), np.sin(angles)
    return (
        np.concatenate((cosine, cosine), axis=1).astype(np.float32),
        np.concatenate((-sine, sine), axis=1).astype(np.float32),
    )


def solution(mesh):
    sections, n_ctx, n = (mesh.shape[a] for a in ("section", "ctx", "tensor"))

    def body(arr, sto, docs_f, docs_b, gain, wq, wk, wv, wo):
        rows, width = arr.shape[1:]
        depth, qw = wq.shape[1:]
        odepth, ow = wo.shape[1:]
        pair = jnp.stack((docs_f[0], docs_b[0]), axis=0)
        docs_rows = jnp.broadcast_to(pair[:, None, :], (2, 8, rows))
        docs_cols = pair[:, :, None]
        cosine, sine = rope_tables(rows * n_ctx)
        n_pieces = 3 + Q_PIECES + O_PIECES + 2
        hbm = pl.BlockSpec(memory_space=pl.ANY)
        vmem = pl.BlockSpec(memory_space=pltpu.VMEM)
        dma = pltpu.SemaphoreType.DMA
        block = jax.ShapeDtypeStruct((1, rows, width), BF16)

        def kernel(*refs):
            layer_kernel(sections, n_ctx, n, *refs)

        return pl.pallas_call(
            kernel,
            out_shape=(block, block, block),
            in_specs=[hbm, hbm, hbm, vmem, vmem] + [hbm] * 6,
            out_specs=(hbm, hbm, hbm),
            scratch_shapes=[
                pltpu.VMEM((2, n, rows, width), BF16),
                pltpu.VMEM((n_ctx, depth, qw), BF16),
                pltpu.VMEM((n_ctx, depth, 2 * HEAD), BF16),
                pltpu.VMEM((n_ctx, odepth, ow), BF16),
                pltpu.VMEM((2 * rows, n * width), BF16),
                pltpu.VMEM((2 * rows, qw), BF16),
                pltpu.VMEM((2 * rows, qw), BF16),
                pltpu.VMEM((n_ctx, 2, rows, 2 * HEAD), BF16),
                pltpu.VMEM((n_ctx, 2, 8, rows), jnp.int32),
                pltpu.VMEM((rows, HEAD), F32),
                pltpu.VMEM((rows, HEAD), F32),
                pltpu.VMEM((n, 2 * rows, width), F32),
                pltpu.VMEM((n, 2 * rows, width), BF16),
                pltpu.VMEM((n, 2 * rows, width), BF16),
                pltpu.VMEM((n, 2 * rows, width), BF16),
                pltpu.VMEM((2 * rows, width), BF16),
                dma((8 + 2 * SUM_PARTS,)),
                dma((2,)),
                dma((2,)),
                dma((2, 2, n - 1)),
                dma((2, 2, n - 1)),
                dma((n_pieces,)),
                dma((n_pieces,)),
                dma((n_pieces,)),
                dma((n_pieces,)),
                dma((n_pieces,)),
                dma((n_pieces,)),
                dma((2, n, 2 * SUM_PARTS)),
                dma((2, n, 2 * SUM_PARTS)),
            ],
            compiler_params=pltpu.CompilerParams(
                collective_id=0, has_side_effects=True, vmem_limit_bytes=62 * 1024 * 1024
            ),
            cost_estimate=pl.CostEstimate(
                flops=2 * 2 * rows * n * width * (2 * qw + 2 * HEAD),
                bytes_accessed=16 * 1024 * 1024,
                transcendentals=8 * 2 * rows * 768,
            ),
            name="relay_layer",
        )(arr, sto, docs_rows, docs_cols, gain, wq, wk, wv, wo, cosine, sine)

    return jax.shard_map(
        body,
        mesh=mesh,
        in_specs=(
            P("section", "ctx", "tensor"),
            P("section", "ctx", "tensor"),
            P("section", "ctx"),
            P("section", "ctx"),
            P("section", None),
            P("section", "ctx", "tensor"),
            P("section", "ctx", "tensor"),
            P("section", "ctx", "tensor"),
            P("section", "tensor", "ctx"),
        ),
        out_specs=(
            P("section", "ctx", "tensor"),
            P("section", "ctx", "tensor"),
            P("section", "ctx", "tensor"),
        ),
        check_vma=False,
    )
```

```python
import math

import jax
import jax.numpy as jnp
import numpy as np
from jax import lax
from jax.experimental import pallas as pl
from jax.experimental.pallas import tpu as pltpu
from jax.sharding import PartitionSpec as P

HEAD = 128
DOC_MOST = 512
norm_epsilon = 1e-05
rope_base = 500000.0
MESH = pl.DeviceIdType.MESH
F32 = jnp.float32
BF16 = jnp.bfloat16
Q_PIECES = 4
O_PIECES = 4
SUM_PARTS = 2


def layer_kernel(
    sections,
    n_ctx,
    n,
    arr,
    sto,
    docs_rows,
    docs_cols,
    gain,
    wq,
    wk,
    wv,
    wo,
    cos_all,
    sin_all,
    out_f,
    out_s,
    out_b,
    xg,
    wq_g,
    wkv_g,
    wo_g,
    normed,
    qs,
    mixed,
    kv_g,
    docs_g,
    cos_t,
    sin_t,
    pf,
    rs_out,
    rl,
    rr,
    res,
    local_sem,
    y_s,
    y_r,
    ag_s,
    ag_r,
    x_s,
    x_r,
    c_s,
    c_r,
    f_s,
    f_r,
    rs_s,
    rs_r,
):
    s = lax.axis_index("section")
    i = lax.axis_index("ctx")
    t = lax.axis_index("tensor")
    rows = arr.shape[1]
    width = arr.shape[2]
    depth = wq.shape[1]
    heads = wq.shape[2] // HEAD
    half = sections // 2
    parts_each = SUM_PARTS
    sum_rows = rows // SUM_PARTS
    partner = lax.rem(s + half, sections)
    across = lax.rem(i + n_ctx // 2, n_ctx)
    sibling = i + 1 - 2 * lax.rem(i, 2)
    has_left = t > 0
    has_right = t < n - 1

    barrier = pltpu.get_barrier_semaphore()
    pl.semaphore_signal(barrier, inc=1, device_id={"section": partner}, device_id_type=MESH)
    pl.semaphore_signal(barrier, inc=1, device_id={"ctx": across}, device_id_type=MESH)
    pl.semaphore_signal(barrier, inc=1, device_id={"ctx": sibling}, device_id_type=MESH)

    @pl.when(has_left)
    def _():
        pl.semaphore_signal(barrier, inc=1, device_id={"tensor": t - 1}, device_id_type=MESH)

    @pl.when(has_right)
    def _():
        pl.semaphore_signal(barrier, inc=1, device_id={"tensor": t + 1}, device_id_type=MESH)

    q_rows = depth // Q_PIECES
    o_rows = wo.shape[1] // O_PIECES
    locals_ = [
        (arr.at[0], xg.at[0, t]),
        (wk.at[0], wkv_g.at[i, :, pl.ds(0, HEAD)]),
        (wv.at[0], wkv_g.at[i, :, pl.ds(HEAD, HEAD)]),
        (wq.at[0], wq_g.at[i]),
        (wo.at[0], wo_g.at[i]),
        (docs_rows, docs_g.at[i]),
        (cos_all.at[pl.ds(pl.multiple_of(i * rows, rows), rows)], cos_t),
        (sin_all.at[pl.ds(pl.multiple_of(i * rows, rows), rows)], sin_t),
    ]
    local_copies = [
        pltpu.make_async_copy(a, b, local_sem.at[k]) for k, (a, b) in enumerate(locals_)
    ]
    for copy in local_copies:
        copy.start()

    pl.semaphore_wait(
        barrier, 3 + has_left.astype(jnp.int32) + has_right.astype(jnp.int32)
    )

    def remote(src, dst, send, recv, where):
        return pltpu.make_async_remote_copy(
            src_ref=src,
            dst_ref=dst,
            send_sem=send,
            recv_sem=recv,
            device_id=where,
            device_id_type=MESH,
        )

    pieces = [
        (docs_rows, lambda j: docs_g.at[j]),
        (wk.at[0], lambda j: wkv_g.at[j, :, pl.ds(0, HEAD)]),
        (wv.at[0], lambda j: wkv_g.at[j, :, pl.ds(HEAD, HEAD)]),
    ]
    for k in range(Q_PIECES):
        part = pl.ds(k * q_rows, q_rows)
        pieces.append((wq.at[0, part], lambda j, part=part: wq_g.at[j, part]))
    first_o = len(pieces)
    for k in range(O_PIECES):
        part = pl.ds(k * o_rows, o_rows)
        pieces.append((wo.at[0, part], lambda j, part=part: wo_g.at[j, part]))
    kv_piece = len(pieces)
    for b in range(2):
        pieces.append((kv_g.at[i, b], lambda j, b=b: kv_g.at[j, b]))

    x_half = i // (n_ctx // 2)
    first_own = jnp.where(x_half == 0, 0, n_ctx - 1)
    first_far = jnp.where(x_half == 0, n_ctx - 1, 0)
    second_own = jnp.where(x_half == 0, 1, n_ctx - 2)
    second_far = jnp.where(x_half == 0, n_ctx - 2, 1)
    per_slot = O_PIECES // 2

    def out_piece(p, far):
        k, w = (p - first_o) // per_slot, (p - first_o) % per_slot
        place = pl.multiple_of((lax.rem(i, 2) * per_slot + w) * o_rows, o_rows)
        slot = ((first_own, second_own), (first_far, second_far))[far][k]
        return wo_g.at[slot, pl.ds(place, o_rows)]

    def is_out(p):
        return first_o <= p < kv_piece

    def to_across(p):
        if is_out(p):
            ref = out_piece(p, 0)
            return remote(ref, ref, x_s.at[p], x_r.at[p], {"ctx": across})
        src, slot = pieces[p]
        return remote(src, slot(i), x_s.at[p], x_r.at[p], {"ctx": across})

    def to_sibling(p):
        src, slot = pieces[p]
        return remote(src, slot(i), c_s.at[p], c_r.at[p], {"ctx": sibling})

    def passed_on(p):
        if is_out(p):
            ref = out_piece(p, 1)
            return remote(ref, ref, f_s.at[p], f_r.at[p], {"ctx": sibling})
        _, slot = pieces[p]
        return remote(slot(across), slot(across), f_s.at[p], f_r.at[p], {"ctx": sibling})

    def pass_on(p):
        to_across(p).wait_recv()
        passed_on(p).start()

    def arrived(p):
        to_sibling(p).wait_recv()
        passed_on(p).wait_recv()

    def ag_right(b, r):
        j = jnp.maximum(t - r, 0)
        src = arr.at[0] if (b == 0 and r == 0) else xg.at[b, j]
        return remote(src, xg.at[b, j], ag_s.at[0, b, r], ag_r.at[0, b, r], {"tensor": t + 1})

    def ag_left(b, r):
        j = jnp.minimum(t + r, n - 1)
        src = arr.at[0] if (b == 0 and r == 0) else xg.at[b, j]
        return remote(src, xg.at[b, j], ag_s.at[1, b, r], ag_r.at[1, b, r], {"tensor": t - 1})

    def sends_right(r):
        return has_right & (t >= r)

    def sends_left(r):
        return has_left & (t + r <= n - 1)

    def ag_start(b, r):
        @pl.when(sends_right(r))
        def _():
            ag_right(b, r).start()

        @pl.when(sends_left(r))
        def _():
            ag_left(b, r).start()

    def ag_wait(b, r):
        @pl.when(t - 1 - r >= 0)
        def _():
            ag_right(b, r).wait_recv()

        @pl.when(t + 1 + r <= n - 1)
        def _():
            ag_left(b, r).wait_recv()

    fetch = remote(sto.at[0], xg.at[1, t], y_s.at[0], y_r.at[0], {"section": partner})
    stash = remote(arr.at[0], out_s.at[0], y_s.at[1], y_r.at[1], {"section": partner})

    fetch.start()
    ag_start(0, 0)
    for p in range(first_o):
        to_across(p).start()
    for p in range(kv_piece):
        to_sibling(p).start()
    fetch.wait_recv()
    ag_start(1, 0)
    stash.start()
    for r in range(n - 2):
        for b in range(2):
            ag_wait(b, r)
            ag_start(b, r + 1)
    def normalize(b):
        def step(k, carry):
            part = pl.ds(pl.multiple_of(k * 16, 16), 16)
            square = jnp.zeros((16, 1), F32)
            for j in range(n):
                v = xg[b, j, part, :].astype(F32)
                square = square + jnp.sum(v * v, axis=1, keepdims=True)
            factor = lax.rsqrt(square * (1.0 / (n * width)) + norm_epsilon)
            place = pl.ds(pl.multiple_of(b * rows + k * 16, 16), 16)
            for j in range(n):
                v = xg[b, j, part, :].astype(F32)
                g = gain[:, j * width : (j + 1) * width].astype(F32)
                normed[place, j * width : (j + 1) * width] = (v * factor * g).astype(BF16)
            return carry

        lax.fori_loop(0, rows // 16, step, 0)

    def rotated(v):
        return v * cos_t[...] + pltpu.roll(v, HEAD // 2, 1) * sin_t[...]

    def project_keys(b):
        own = slice(b * rows, (b + 1) * rows)
        k_and_v = jnp.zeros((rows, 2 * HEAD), F32)
        for j in range(n_ctx):
            k_and_v = k_and_v + jnp.dot(
                normed[own, j * depth : (j + 1) * depth], wkv_g[j], preferred_element_type=F32
            )
        kv_g[i, b, :, :HEAD] = rotated(k_and_v[:, :HEAD]).astype(BF16)
        kv_g[i, b, :, HEAD:] = k_and_v[:, HEAD:].astype(BF16)
        to_across(kv_piece + b).start()
        to_sibling(kv_piece + b).start()

    def project_queries(b):
        own = slice(b * rows, (b + 1) * rows)

        def q_step(c, carry):
            cols = pl.ds(pl.multiple_of(c * 2 * HEAD, 2 * HEAD), 2 * HEAD)
            acc = jnp.zeros((rows, 2 * HEAD), F32)
            for j in range(n_ctx):
                acc = acc + jnp.dot(
                    normed[own, j * depth : (j + 1) * depth],
                    wq_g[j, :, cols],
                    preferred_element_type=F32,
                )
            for h in range(2):
                place = pl.ds(pl.multiple_of((c * 2 + h) * HEAD, HEAD), HEAD)
                qs[own, place] = rotated(acc[:, h * HEAD : (h + 1) * HEAD]).astype(BF16)
            return carry

        lax.fori_loop(0, heads // 2, q_step, 0)

    blocks = min(n_ctx, -(-(DOC_MOST - 1) // rows) + 1)
    start = jnp.maximum(i - (blocks - 1), 0)
    keys = blocks * rows

    def attend(b):
        q_pos = i * rows + lax.broadcasted_iota(jnp.int32, (rows, keys), 0)
        k_pos = start * rows + lax.broadcasted_iota(jnp.int32, (rows, keys), 1)
        key_docs = jnp.concatenate([docs_g[start + j, b] for j in range(blocks)], axis=1)
        allowed = (k_pos <= q_pos) & (docs_cols[b] == key_docs[:1])
        k_b = jnp.concatenate([kv_g[start + j, b, :, :HEAD] for j in range(blocks)], axis=0)
        v_b = jnp.concatenate([kv_g[start + j, b, :, HEAD:] for j in range(blocks)], axis=0)

        def head_step(h, carry):
            place = pl.ds(pl.multiple_of(h * HEAD, HEAD), HEAD)
            q_h = qs[b * rows : (b + 1) * rows, place]
            scores = lax.dot_general(
                q_h, k_b, (((1,), (1,)), ((), ())), preferred_element_type=F32
            ) * (1.0 / math.sqrt(HEAD))
            masked = jnp.where(allowed, scores, -jnp.inf)
            peak = jnp.max(masked, axis=1, keepdims=True)
            weights = jnp.exp(masked - peak)
            total = jnp.sum(weights, axis=1, keepdims=True)
            mix = jnp.dot(weights.astype(BF16), v_b, preferred_element_type=F32)
            mixed[b * rows : (b + 1) * rows, place] = (mix / total).astype(BF16)
            return carry

        lax.fori_loop(0, heads, head_step, 0)

    n_half = n // 2
    near = x_half * n_half

    def project(b, base, count):
        own = slice(b * rows, (b + 1) * rows)

        def step(c, carry):
            d = base + c // (width // 256)
            cols = pl.ds(pl.multiple_of(lax.rem(c, width // 256) * 256, 256), 256)
            pf[d, own, cols] = jnp.dot(mixed[own, :], wo_g[d, :, cols], preferred_element_type=F32)
            return carry

        lax.fori_loop(0, count * (width // 256), step, 0)

    def part_of(m):
        return pl.ds(m * sum_rows, sum_rows)

    def rs_right(d, m):
        part = part_of(m)
        return remote(
            rs_out.at[d, part], rl.at[d, part], rs_s.at[0, d, m], rs_r.at[0, d, m], {"tensor": t + 1}
        )

    def rs_left(d, m):
        part = part_of(m)
        return remote(
            rs_out.at[d, part], rr.at[d, part], rs_s.at[1, d, m], rs_r.at[1, d, m], {"tensor": t - 1}
        )

    def pieces_of(b):
        return range(b * parts_each, (b + 1) * parts_each)

    def first_sends(b, base, count):
        for q in range(count):
            low, high = base + q, base + count - 1 - q

            @pl.when((t == n - 1) & (low < t))
            def _():
                for m in pieces_of(b):
                    rs_out[low, part_of(m), :] = pf[low, part_of(m), :].astype(BF16)
                    rs_left(low, m).start()

            @pl.when((t == 0) & (high > t))
            def _():
                for m in pieces_of(b):
                    rs_out[high, part_of(m), :] = pf[high, part_of(m), :].astype(BF16)
                    rs_right(high, m).start()

    def middle_sends(b, base, count, q):
        low, high = base + q, base + count - 1 - q

        @pl.when((t < n - 1) & (low < t))
        def _():
            for m in pieces_of(b):
                rs_left(low, m).wait_recv()
                rs_out[low, part_of(m), :] = (
                    pf[low, part_of(m), :] + rr[low, part_of(m), :].astype(F32)
                ).astype(BF16)
                rs_left(low, m).start()

        @pl.when((t > 0) & (high > t))
        def _():
            for m in pieces_of(b):
                rs_right(high, m).wait_recv()
                rs_out[high, part_of(m), :] = (
                    pf[high, part_of(m), :] + rl[high, part_of(m), :].astype(F32)
                ).astype(BF16)
                rs_right(high, m).start()

    for copy in local_copies:
        copy.wait()
    ag_wait(0, n - 2)
    normalize(0)
    for p in range(first_o):
        pass_on(p)
    for p in range(first_o):
        arrived(p)
    project_keys(0)
    for p in range(first_o, kv_piece):
        to_sibling(p).wait_recv()
    for p in range(first_o, first_o + per_slot):
        to_across(p).start()
    project_queries(0)
    pass_on(kv_piece)
    arrived(kv_piece)
    attend(0)
    project(0, near, n_half)
    first_sends(0, near, n_half)

    ag_wait(1, n - 2)
    normalize(1)
    project_keys(1)
    for p in range(first_o + per_slot, kv_piece):
        to_across(p).start()
    project_queries(1)
    pass_on(kv_piece + 1)
    arrived(kv_piece + 1)
    attend(1)
    project(1, near, n_half)
    first_sends(1, near, n_half)

    for p in range(first_o, first_o + per_slot):
        pass_on(p)
    for q in range(n_half):
        middle_sends(0, near, n_half, q)
    for p in range(first_o, first_o + per_slot):
        passed_on(p).wait_recv()
    for b in range(2):
        project(b, first_far, 1)
        first_sends(b, first_far, 1)
    middle_sends(1, near, n_half, 0)
    for p in range(first_o + per_slot, kv_piece):
        pass_on(p)
    for q in range(1, n_half):
        middle_sends(1, near, n_half, q)
    for p in range(first_o + per_slot, kv_piece):
        passed_on(p).wait_recv()
    for b in range(2):
        project(b, second_far, 1)
        first_sends(b, second_far, 1)
    for d in (first_far, second_far):
        for b in range(2):
            middle_sends(b, d, 1, 0)

    outs = []
    for m in range(2 * parts_each):
        b, k = m // parts_each, m % parts_each
        part = part_of(m)

        @pl.when(has_left)
        def _():
            rs_right(t, m).wait_recv()
            pf[t, part, :] = pf[t, part, :] + rl[t, part, :].astype(F32)

        @pl.when(has_right)
        def _():
            rs_left(t, m).wait_recv()
            pf[t, part, :] = pf[t, part, :] + rr[t, part, :].astype(F32)

        own = pl.ds(k * sum_rows, sum_rows)
        res[part, :] = (xg[b, t, own, :].astype(F32) + pf[t, part, :]).astype(BF16)
        out = pltpu.make_async_copy(
            res.at[part], (out_f, out_b)[b].at[0, own], local_sem.at[len(locals_) + m]
        )
        out.start()
        outs.append(out)
    for out in outs:
        out.wait()

    stash.wait_recv()
    fetch.wait_send()
    stash.wait_send()
    for p in range(len(pieces)):
        to_across(p).wait_send()
        to_sibling(p).wait_send()
        passed_on(p).wait_send()
    for r in range(n - 1):
        for b in range(2):

            @pl.when(sends_right(r))
            def _():
                ag_right(b, r).wait_send()

            @pl.when(sends_left(r))
            def _():
                ag_left(b, r).wait_send()

    for d in range(n):

        @pl.when(d > t)
        def _():
            for m in range(2 * parts_each):
                rs_right(d, m).wait_send()

        @pl.when(d < t)
        def _():
            for m in range(2 * parts_each):
                rs_left(d, m).wait_send()


def rope_tables(tokens):
    exponent = np.arange(HEAD // 2, dtype=np.float64) * (2.0 / HEAD)
    angles = np.arange(tokens, dtype=np.float64)[:, None] * rope_base ** -exponent[None, :]
    cosine, sine = np.cos(angles), np.sin(angles)
    return (
        np.concatenate((cosine, cosine), axis=1).astype(np.float32),
        np.concatenate((-sine, sine), axis=1).astype(np.float32),
    )


def solution(mesh):
    sections, n_ctx, n = (mesh.shape[a] for a in ("section", "ctx", "tensor"))

    def body(arr, sto, docs_f, docs_b, gain, wq, wk, wv, wo):
        rows, width = arr.shape[1:]
        depth, qw = wq.shape[1:]
        odepth, ow = wo.shape[1:]
        pair = jnp.stack((docs_f[0], docs_b[0]), axis=0)
        docs_rows = jnp.broadcast_to(pair[:, None, :], (2, 8, rows))
        docs_cols = pair[:, :, None]
        cosine, sine = rope_tables(rows * n_ctx)
        n_pieces = 3 + Q_PIECES + O_PIECES + 2
        hbm = pl.BlockSpec(memory_space=pl.ANY)
        vmem = pl.BlockSpec(memory_space=pltpu.VMEM)
        dma = pltpu.SemaphoreType.DMA
        block = jax.ShapeDtypeStruct((1, rows, width), BF16)

        def kernel(*refs):
            layer_kernel(sections, n_ctx, n, *refs)

        return pl.pallas_call(
            kernel,
            out_shape=(block, block, block),
            in_specs=[hbm, hbm, hbm, vmem, vmem] + [hbm] * 6,
            out_specs=(hbm, hbm, hbm),
            scratch_shapes=[
                pltpu.VMEM((2, n, rows, width), BF16),
                pltpu.VMEM((n_ctx, depth, qw), BF16),
                pltpu.VMEM((n_ctx, depth, 2 * HEAD), BF16),
                pltpu.VMEM((n_ctx, odepth, ow), BF16),
                pltpu.VMEM((2 * rows, n * width), BF16),
                pltpu.VMEM((2 * rows, qw), BF16),
                pltpu.VMEM((2 * rows, qw), BF16),
                pltpu.VMEM((n_ctx, 2, rows, 2 * HEAD), BF16),
                pltpu.VMEM((n_ctx, 2, 8, rows), jnp.int32),
                pltpu.VMEM((rows, HEAD), F32),
                pltpu.VMEM((rows, HEAD), F32),
                pltpu.VMEM((n, 2 * rows, width), F32),
                pltpu.VMEM((n, 2 * rows, width), BF16),
                pltpu.VMEM((n, 2 * rows, width), BF16),
                pltpu.VMEM((n, 2 * rows, width), BF16),
                pltpu.VMEM((2 * rows, width), BF16),
                dma((8 + 2 * SUM_PARTS,)),
                dma((2,)),
                dma((2,)),
                dma((2, 2, n - 1)),
                dma((2, 2, n - 1)),
                dma((n_pieces,)),
                dma((n_pieces,)),
                dma((n_pieces,)),
                dma((n_pieces,)),
                dma((n_pieces,)),
                dma((n_pieces,)),
                dma((2, n, 2 * SUM_PARTS)),
                dma((2, n, 2 * SUM_PARTS)),
            ],
            compiler_params=pltpu.CompilerParams(
                collective_id=0, has_side_effects=True, vmem_limit_bytes=62 * 1024 * 1024
            ),
            cost_estimate=pl.CostEstimate(
                flops=2 * 2 * rows * n * width * (2 * qw + 2 * HEAD),
                bytes_accessed=16 * 1024 * 1024,
                transcendentals=8 * 2 * rows * 768,
            ),
            name="relay_layer",
        )(arr, sto, docs_rows, docs_cols, gain, wq, wk, wv, wo, cosine, sine)

    return jax.shard_map(
        body,
        mesh=mesh,
        in_specs=(
            P("section", "ctx", "tensor"),
            P("section", "ctx", "tensor"),
            P("section", "ctx"),
            P("section", "ctx"),
            P("section", None),
            P("section", "ctx", "tensor"),
            P("section", "ctx", "tensor"),
            P("section", "ctx", "tensor"),
            P("section", "tensor", "ctx"),
        ),
        out_specs=(
            P("section", "ctx", "tensor"),
            P("section", "ctx", "tensor"),
            P("section", "ctx", "tensor"),
        ),
        check_vma=False,
    )
```

```python
import math

import jax
import jax.numpy as jnp
import numpy as np
from jax import lax
from jax.experimental import pallas as pl
from jax.experimental.pallas import tpu as pltpu
from jax.sharding import PartitionSpec as P

HEAD = 128
DOC_MOST = 512
norm_epsilon = 1e-05
rope_base = 500000.0
MESH = pl.DeviceIdType.MESH
F32 = jnp.float32
BF16 = jnp.bfloat16
Q_PIECES = 4
O_PIECES = 4
SUM_PARTS = 2


def layer_kernel(
    sections,
    n_ctx,
    n,
    arr,
    sto,
    docs_rows,
    docs_cols,
    gain,
    wq,
    wk,
    wv,
    wo,
    cos_all,
    sin_all,
    out_f,
    out_s,
    out_b,
    xg,
    wq_g,
    wkv_g,
    wo_g,
    normed,
    qs,
    mixed,
    kv_g,
    docs_g,
    cos_t,
    sin_t,
    pf,
    rs_out,
    rl,
    rr,
    res,
    local_sem,
    y_s,
    y_r,
    ag_s,
    ag_r,
    x_s,
    x_r,
    c_s,
    c_r,
    f_s,
    f_r,
    rs_s,
    rs_r,
):
    s = lax.axis_index("section")
    i = lax.axis_index("ctx")
    t = lax.axis_index("tensor")
    rows = arr.shape[1]
    width = arr.shape[2]
    depth = wq.shape[1]
    heads = wq.shape[2] // HEAD
    half = sections // 2
    parts_each = SUM_PARTS
    sum_rows = rows // SUM_PARTS
    partner = lax.rem(s + half, sections)
    across = lax.rem(i + n_ctx // 2, n_ctx)
    sibling = i + 1 - 2 * lax.rem(i, 2)
    has_left = t > 0
    has_right = t < n - 1

    barrier = pltpu.get_barrier_semaphore()
    pl.semaphore_signal(barrier, inc=1, device_id={"section": partner}, device_id_type=MESH)
    pl.semaphore_signal(barrier, inc=1, device_id={"ctx": across}, device_id_type=MESH)
    pl.semaphore_signal(barrier, inc=1, device_id={"ctx": sibling}, device_id_type=MESH)

    @pl.when(has_left)
    def _():
        pl.semaphore_signal(barrier, inc=1, device_id={"tensor": t - 1}, device_id_type=MESH)

    @pl.when(has_right)
    def _():
        pl.semaphore_signal(barrier, inc=1, device_id={"tensor": t + 1}, device_id_type=MESH)

    q_rows = depth // Q_PIECES
    o_rows = wo.shape[1] // O_PIECES
    locals_ = [
        (arr.at[0], xg.at[0, t]),
        (wk.at[0], wkv_g.at[i, :, pl.ds(0, HEAD)]),
        (wv.at[0], wkv_g.at[i, :, pl.ds(HEAD, HEAD)]),
        (wq.at[0], wq_g.at[i]),
        (wo.at[0], wo_g.at[i]),
        (docs_rows, docs_g.at[i]),
        (cos_all.at[pl.ds(pl.multiple_of(i * rows, rows), rows)], cos_t),
        (sin_all.at[pl.ds(pl.multiple_of(i * rows, rows), rows)], sin_t),
    ]
    local_copies = [
        pltpu.make_async_copy(a, b, local_sem.at[k]) for k, (a, b) in enumerate(locals_)
    ]
    for copy in local_copies:
        copy.start()

    pl.semaphore_wait(
        barrier, 3 + has_left.astype(jnp.int32) + has_right.astype(jnp.int32)
    )

    def remote(src, dst, send, recv, where):
        return pltpu.make_async_remote_copy(
            src_ref=src,
            dst_ref=dst,
            send_sem=send,
            recv_sem=recv,
            device_id=where,
            device_id_type=MESH,
        )

    pieces = [
        (docs_rows, lambda j: docs_g.at[j]),
        (wk.at[0], lambda j: wkv_g.at[j, :, pl.ds(0, HEAD)]),
        (wv.at[0], lambda j: wkv_g.at[j, :, pl.ds(HEAD, HEAD)]),
    ]
    for k in range(Q_PIECES):
        part = pl.ds(k * q_rows, q_rows)
        pieces.append((wq.at[0, part], lambda j, part=part: wq_g.at[j, part]))
    first_o = len(pieces)
    for k in range(O_PIECES):
        part = pl.ds(k * o_rows, o_rows)
        pieces.append((wo.at[0, part], lambda j, part=part: wo_g.at[j, part]))
    kv_piece = len(pieces)
    for b in range(2):
        pieces.append((kv_g.at[i, b], lambda j, b=b: kv_g.at[j, b]))

    def to_across(p):
        src, slot = pieces[p]
        return remote(src, slot(i), x_s.at[p], x_r.at[p], {"ctx": across})

    def to_sibling(p):
        src, slot = pieces[p]
        return remote(src, slot(i), c_s.at[p], c_r.at[p], {"ctx": sibling})

    def passed_on(p):
        _, slot = pieces[p]
        return remote(slot(across), slot(across), f_s.at[p], f_r.at[p], {"ctx": sibling})

    def pass_on(p):
        to_across(p).wait_recv()
        passed_on(p).start()

    def arrived(p):
        to_sibling(p).wait_recv()
        passed_on(p).wait_recv()

    def ag_right(b, r):
        j = jnp.maximum(t - r, 0)
        src = arr.at[0] if (b == 0 and r == 0) else xg.at[b, j]
        return remote(src, xg.at[b, j], ag_s.at[0, b, r], ag_r.at[0, b, r], {"tensor": t + 1})

    def ag_left(b, r):
        j = jnp.minimum(t + r, n - 1)
        src = arr.at[0] if (b == 0 and r == 0) else xg.at[b, j]
        return remote(src, xg.at[b, j], ag_s.at[1, b, r], ag_r.at[1, b, r], {"tensor": t - 1})

    def sends_right(r):
        return has_right & (t >= r)

    def sends_left(r):
        return has_left & (t + r <= n - 1)

    def ag_start(b, r):
        @pl.when(sends_right(r))
        def _():
            ag_right(b, r).start()

        @pl.when(sends_left(r))
        def _():
            ag_left(b, r).start()

    def ag_wait(b, r):
        @pl.when(t - 1 - r >= 0)
        def _():
            ag_right(b, r).wait_recv()

        @pl.when(t + 1 + r <= n - 1)
        def _():
            ag_left(b, r).wait_recv()

    fetch = remote(sto.at[0], xg.at[1, t], y_s.at[0], y_r.at[0], {"section": partner})
    stash = remote(arr.at[0], out_s.at[0], y_s.at[1], y_r.at[1], {"section": partner})

    fetch.start()
    ag_start(0, 0)
    for p in range(first_o):
        to_across(p).start()
    for p in range(kv_piece):
        to_sibling(p).start()
    fetch.wait_recv()
    ag_start(1, 0)
    stash.start()
    for r in range(n - 2):
        for b in range(2):
            ag_wait(b, r)
            ag_start(b, r + 1)
    def normalize(b):
        def step(k, carry):
            part = pl.ds(pl.multiple_of(k * 16, 16), 16)
            square = jnp.zeros((16, 1), F32)
            for j in range(n):
                v = xg[b, j, part, :].astype(F32)
                square = square + jnp.sum(v * v, axis=1, keepdims=True)
            factor = lax.rsqrt(square * (1.0 / (n * width)) + norm_epsilon)
            place = pl.ds(pl.multiple_of(b * rows + k * 16, 16), 16)
            for j in range(n):
                v = xg[b, j, part, :].astype(F32)
                g = gain[:, j * width : (j + 1) * width].astype(F32)
                normed[place, j * width : (j + 1) * width] = (v * factor * g).astype(BF16)
            return carry

        lax.fori_loop(0, rows // 16, step, 0)

    def rotated(v):
        return v * cos_t[...] + pltpu.roll(v, HEAD // 2, 1) * sin_t[...]

    def project_keys(b):
        own = slice(b * rows, (b + 1) * rows)
        k_and_v = jnp.zeros((rows, 2 * HEAD), F32)
        for j in range(n_ctx):
            k_and_v = k_and_v + jnp.dot(
                normed[own, j * depth : (j + 1) * depth], wkv_g[j], preferred_element_type=F32
            )
        kv_g[i, b, :, :HEAD] = rotated(k_and_v[:, :HEAD]).astype(BF16)
        kv_g[i, b, :, HEAD:] = k_and_v[:, HEAD:].astype(BF16)
        to_across(kv_piece + b).start()
        to_sibling(kv_piece + b).start()

    def project_queries(b):
        own = slice(b * rows, (b + 1) * rows)

        def q_step(c, carry):
            cols = pl.ds(pl.multiple_of(c * 2 * HEAD, 2 * HEAD), 2 * HEAD)
            acc = jnp.zeros((rows, 2 * HEAD), F32)
            for j in range(n_ctx):
                acc = acc + jnp.dot(
                    normed[own, j * depth : (j + 1) * depth],
                    wq_g[j, :, cols],
                    preferred_element_type=F32,
                )
            for h in range(2):
                place = pl.ds(pl.multiple_of((c * 2 + h) * HEAD, HEAD), HEAD)
                qs[own, place] = rotated(acc[:, h * HEAD : (h + 1) * HEAD]).astype(BF16)
            return carry

        lax.fori_loop(0, heads // 2, q_step, 0)

    blocks = min(n_ctx, -(-(DOC_MOST - 1) // rows) + 1)
    start = jnp.maximum(i - (blocks - 1), 0)
    keys = blocks * rows

    def attend(b):
        q_pos = i * rows + lax.broadcasted_iota(jnp.int32, (rows, keys), 0)
        k_pos = start * rows + lax.broadcasted_iota(jnp.int32, (rows, keys), 1)
        key_docs = jnp.concatenate([docs_g[start + j, b] for j in range(blocks)], axis=1)
        allowed = (k_pos <= q_pos) & (docs_cols[b] == key_docs[:1])
        k_b = jnp.concatenate([kv_g[start + j, b, :, :HEAD] for j in range(blocks)], axis=0)
        v_b = jnp.concatenate([kv_g[start + j, b, :, HEAD:] for j in range(blocks)], axis=0)

        def head_step(h, carry):
            place = pl.ds(pl.multiple_of(h * HEAD, HEAD), HEAD)
            q_h = qs[b * rows : (b + 1) * rows, place]
            scores = lax.dot_general(
                q_h, k_b, (((1,), (1,)), ((), ())), preferred_element_type=F32
            ) * (1.0 / math.sqrt(HEAD))
            masked = jnp.where(allowed, scores, -jnp.inf)
            peak = jnp.max(masked, axis=1, keepdims=True)
            weights = jnp.exp(masked - peak)
            total = jnp.sum(weights, axis=1, keepdims=True)
            mix = jnp.dot(weights.astype(BF16), v_b, preferred_element_type=F32)
            mixed[b * rows : (b + 1) * rows, place] = (mix / total).astype(BF16)
            return carry

        lax.fori_loop(0, heads, head_step, 0)

    n_half = n // 2
    x_half = i // (n_ctx // 2)
    near = x_half * n_half
    far = (1 - x_half) * n_half

    def project(b, base):
        own = slice(b * rows, (b + 1) * rows)

        def step(c, carry):
            d = base + c // (width // 256)
            cols = pl.ds(pl.multiple_of(lax.rem(c, width // 256) * 256, 256), 256)
            pf[d, own, cols] = jnp.dot(mixed[own, :], wo_g[d, :, cols], preferred_element_type=F32)
            return carry

        lax.fori_loop(0, n_half * (width // 256), step, 0)

    def part_of(m):
        return pl.ds(m * sum_rows, sum_rows)

    def rs_right(d, m):
        part = part_of(m)
        return remote(
            rs_out.at[d, part], rl.at[d, part], rs_s.at[0, d, m], rs_r.at[0, d, m], {"tensor": t + 1}
        )

    def rs_left(d, m):
        part = part_of(m)
        return remote(
            rs_out.at[d, part], rr.at[d, part], rs_s.at[1, d, m], rs_r.at[1, d, m], {"tensor": t - 1}
        )

    def pieces_of(b):
        return range(b * parts_each, (b + 1) * parts_each)

    def first_sends(b, base):
        for q in range(n_half):
            low, high = base + q, base + n_half - 1 - q

            @pl.when((t == n - 1) & (low < t))
            def _():
                for m in pieces_of(b):
                    rs_out[low, part_of(m), :] = pf[low, part_of(m), :].astype(BF16)
                    rs_left(low, m).start()

            @pl.when((t == 0) & (high > t))
            def _():
                for m in pieces_of(b):
                    rs_out[high, part_of(m), :] = pf[high, part_of(m), :].astype(BF16)
                    rs_right(high, m).start()

    def middle_sends(b, base, q):
        low, high = base + q, base + n_half - 1 - q

        @pl.when((t < n - 1) & (low < t))
        def _():
            for m in pieces_of(b):
                rs_left(low, m).wait_recv()
                rs_out[low, part_of(m), :] = (
                    pf[low, part_of(m), :] + rr[low, part_of(m), :].astype(F32)
                ).astype(BF16)
                rs_left(low, m).start()

        @pl.when((t > 0) & (high > t))
        def _():
            for m in pieces_of(b):
                rs_right(high, m).wait_recv()
                rs_out[high, part_of(m), :] = (
                    pf[high, part_of(m), :] + rl[high, part_of(m), :].astype(F32)
                ).astype(BF16)
                rs_right(high, m).start()

    for copy in local_copies:
        copy.wait()
    ag_wait(0, n - 2)
    normalize(0)
    for p in range(first_o):
        pass_on(p)
    for p in range(first_o):
        arrived(p)
    project_keys(0)
    project_queries(0)
    pass_on(kv_piece)
    for p in range(first_o, first_o + O_PIECES // 2):
        to_across(p).start()
    arrived(kv_piece)
    attend(0)
    for p in range(first_o, kv_piece):
        to_sibling(p).wait_recv()
    project(0, near)
    first_sends(0, near)

    ag_wait(1, n - 2)
    normalize(1)
    project_keys(1)
    for p in range(first_o + O_PIECES // 2, kv_piece):
        to_across(p).start()
    project_queries(1)
    pass_on(kv_piece + 1)
    arrived(kv_piece + 1)
    attend(1)
    project(1, near)
    first_sends(1, near)

    for q in range(n_half):
        middle_sends(0, near, q)
    pass_on(first_o)
    for p in range(first_o + 1, kv_piece):
        pass_on(p)
        if p - first_o - 1 < n_half:
            middle_sends(1, near, p - first_o - 1)
    for p in range(first_o, kv_piece):
        passed_on(p).wait_recv()
    for b in range(2):
        project(b, far)
        first_sends(b, far)
    for b in range(2):
        for q in range(n_half):
            middle_sends(b, far, q)

    outs = []
    for m in range(2 * parts_each):
        b, k = m // parts_each, m % parts_each
        part = part_of(m)

        @pl.when(has_left)
        def _():
            rs_right(t, m).wait_recv()
            pf[t, part, :] = pf[t, part, :] + rl[t, part, :].astype(F32)

        @pl.when(has_right)
        def _():
            rs_left(t, m).wait_recv()
            pf[t, part, :] = pf[t, part, :] + rr[t, part, :].astype(F32)

        own = pl.ds(k * sum_rows, sum_rows)
        res[part, :] = (xg[b, t, own, :].astype(F32) + pf[t, part, :]).astype(BF16)
        out = pltpu.make_async_copy(
            res.at[part], (out_f, out_b)[b].at[0, own], local_sem.at[len(locals_) + m]
        )
        out.start()
        outs.append(out)
    for out in outs:
        out.wait()

    stash.wait_recv()
    fetch.wait_send()
    stash.wait_send()
    for p in range(len(pieces)):
        to_across(p).wait_send()
        to_sibling(p).wait_send()
        passed_on(p).wait_send()
    for r in range(n - 1):
        for b in range(2):

            @pl.when(sends_right(r))
            def _():
                ag_right(b, r).wait_send()

            @pl.when(sends_left(r))
            def _():
                ag_left(b, r).wait_send()

    for d in range(n):

        @pl.when(d > t)
        def _():
            for m in range(2 * parts_each):
                rs_right(d, m).wait_send()

        @pl.when(d < t)
        def _():
            for m in range(2 * parts_each):
                rs_left(d, m).wait_send()


def rope_tables(tokens):
    exponent = np.arange(HEAD // 2, dtype=np.float64) * (2.0 / HEAD)
    angles = np.arange(tokens, dtype=np.float64)[:, None] * rope_base ** -exponent[None, :]
    cosine, sine = np.cos(angles), np.sin(angles)
    return (
        np.concatenate((cosine, cosine), axis=1).astype(np.float32),
        np.concatenate((-sine, sine), axis=1).astype(np.float32),
    )


def solution(mesh):
    sections, n_ctx, n = (mesh.shape[a] for a in ("section", "ctx", "tensor"))

    def body(arr, sto, docs_f, docs_b, gain, wq, wk, wv, wo):
        rows, width = arr.shape[1:]
        depth, qw = wq.shape[1:]
        odepth, ow = wo.shape[1:]
        pair = jnp.stack((docs_f[0], docs_b[0]), axis=0)
        docs_rows = jnp.broadcast_to(pair[:, None, :], (2, 8, rows))
        docs_cols = pair[:, :, None]
        cosine, sine = rope_tables(rows * n_ctx)
        n_pieces = 3 + Q_PIECES + O_PIECES + 2
        hbm = pl.BlockSpec(memory_space=pl.ANY)
        vmem = pl.BlockSpec(memory_space=pltpu.VMEM)
        dma = pltpu.SemaphoreType.DMA
        block = jax.ShapeDtypeStruct((1, rows, width), BF16)

        def kernel(*refs):
            layer_kernel(sections, n_ctx, n, *refs)

        return pl.pallas_call(
            kernel,
            out_shape=(block, block, block),
            in_specs=[hbm, hbm, hbm, vmem, vmem] + [hbm] * 6,
            out_specs=(hbm, hbm, hbm),
            scratch_shapes=[
                pltpu.VMEM((2, n, rows, width), BF16),
                pltpu.VMEM((n_ctx, depth, qw), BF16),
                pltpu.VMEM((n_ctx, depth, 2 * HEAD), BF16),
                pltpu.VMEM((n_ctx, odepth, ow), BF16),
                pltpu.VMEM((2 * rows, n * width), BF16),
                pltpu.VMEM((2 * rows, qw), BF16),
                pltpu.VMEM((2 * rows, qw), BF16),
                pltpu.VMEM((n_ctx, 2, rows, 2 * HEAD), BF16),
                pltpu.VMEM((n_ctx, 2, 8, rows), jnp.int32),
                pltpu.VMEM((rows, HEAD), F32),
                pltpu.VMEM((rows, HEAD), F32),
                pltpu.VMEM((n, 2 * rows, width), F32),
                pltpu.VMEM((n, 2 * rows, width), BF16),
                pltpu.VMEM((n, 2 * rows, width), BF16),
                pltpu.VMEM((n, 2 * rows, width), BF16),
                pltpu.VMEM((2 * rows, width), BF16),
                dma((8 + 2 * SUM_PARTS,)),
                dma((2,)),
                dma((2,)),
                dma((2, 2, n - 1)),
                dma((2, 2, n - 1)),
                dma((n_pieces,)),
                dma((n_pieces,)),
                dma((n_pieces,)),
                dma((n_pieces,)),
                dma((n_pieces,)),
                dma((n_pieces,)),
                dma((2, n, 2 * SUM_PARTS)),
                dma((2, n, 2 * SUM_PARTS)),
            ],
            compiler_params=pltpu.CompilerParams(
                collective_id=0, has_side_effects=True, vmem_limit_bytes=62 * 1024 * 1024
            ),
            cost_estimate=pl.CostEstimate(
                flops=2 * 2 * rows * n * width * (2 * qw + 2 * HEAD),
                bytes_accessed=16 * 1024 * 1024,
                transcendentals=8 * 2 * rows * 768,
            ),
            name="relay_layer",
        )(arr, sto, docs_rows, docs_cols, gain, wq, wk, wv, wo, cosine, sine)

    return jax.shard_map(
        body,
        mesh=mesh,
        in_specs=(
            P("section", "ctx", "tensor"),
            P("section", "ctx", "tensor"),
            P("section", "ctx"),
            P("section", "ctx"),
            P("section", None),
            P("section", "ctx", "tensor"),
            P("section", "ctx", "tensor"),
            P("section", "ctx", "tensor"),
            P("section", "tensor", "ctx"),
        ),
        out_specs=(
            P("section", "ctx", "tensor"),
            P("section", "ctx", "tensor"),
            P("section", "ctx", "tensor"),
        ),
        check_vma=False,
    )
```
